32 devices in a mesh: layer: 4 (over y, core), feat: 8 (over z, x).
Axes of the slice: x: 2, y: 2, z: 4, core: 2. Of those that a mesh axis runs over, the one named last changes fastest.
Arguments:
- resid_stream: bfloat16 [8, 4, 2304], P('feat', 'layer'), may hold values from -6 to 6
- enc_mantissa: bfloat16 [4, 2304, 16384], P('layer', None, 'feat'), may hold values from -96 to 96
- enc_exponent: int32 [4, 18, 128], P('layer', None, 'feat'), may hold values from -11 to -10
- enc_bias: float32 [4, 16384], P('layer', 'feat'), may hold values from -3 to 3
- dec_weight: bfloat16 [10, 16384, 2304], P(None, 'feat', 'layer'), may hold values from -0.046875 to 0.046875
- dec_bias: float32 [4, 2304], P('layer'), may hold values from -3 to 3
Outputs:
- recon: bfloat16 [8, 4, 2304], P('feat', 'layer')
The draws below stay inside these ranges and needn't reach their ends.
All inputs are finite; a program needn't handle non-finite values.
Results may differ from the reference program's by a relative error of at most 0.0044.
Values may be sent and summed in bfloat16 or wider, within the bound.
No kernel may reach another device: no remote copies, remote signals or barrier semaphores. Data moves between devices by JAX's collectives and lax.ppermute only.
A program may use at most 128 MiB of HBM per device.

```python
import jax
import jax.numpy as jnp

D = 2304
F = 16384
LAYERS = 4
BLK = 128
TOKENS = 8
PAIRS = 10


def place_ends(array, own_key, low, high):
    place = [jax.random.randint(jax.random.fold_in(own_key, axis), (), 0, length) for axis, length in enumerate(array.shape)]
    widest = array.shape.index(max(array.shape))
    neighbour = place[:widest] + [(place[widest] + 1) % array.shape[widest]] + place[widest + 1:]
    return array.at[tuple(place)].set(low).at[tuple(neighbour)].set(high)


def shard_levels(stream_key, dims, split, low, largest):
    level = 1.0
    for axis_at, blocks in split:
        steps = jax.random.uniform(jax.random.fold_in(jax.random.fold_in(stream_key, 6), axis_at), (blocks,), jnp.float32, low / len(split), largest / len(split))
        level = level * jnp.repeat(jnp.exp(steps), dims[axis_at] // blocks).reshape((-1,) + (1,) * (len(dims) - 1 - axis_at))
    return level


def scatter_about(stream_key, shape, scale, reach, cuts=(), held_as=jnp.bfloat16):
    result = jax.random.normal(stream_key, shape, jnp.float32) * scale
    if len(cuts) > 0:
        result = shard_levels(stream_key, shape, cuts, -0.22, 0.18) * result
    return jnp.clip(result, min=-reach, max=reach).astype(held_as)


def setup_inputs(seed: int = 0) -> dict:
    key_list = jax.random.split(jax.random.key(seed), 7)
    return {
        "resid_stream": scatter_about(key_list[0], (TOKENS, LAYERS, D), 1.0, 6.0, ((0, 8), (1, 4))),
        "enc_mantissa": scatter_about(key_list[1], (LAYERS, D, F), 16.0, 96.0, ((0, 4), (2, 8))),
        "enc_exponent": place_ends(jax.random.randint(key_list[2], (LAYERS, D // BLK, F // BLK), -11, -9), jax.random.fold_in(key_list[2], 1), -11, (-9) - 1).astype(jnp.int32),
        "enc_bias": scatter_about(key_list[3], (LAYERS, F), 0.5, 3.0, ((0, 4), (1, 8)), jnp.float32),
        "dec_weight": scatter_about(key_list[4], (PAIRS, F, D), F ** -0.5, 0.046875, ((1, 8), (2, 4))),
        "dec_bias": scatter_about(key_list[5], (LAYERS, D), 0.5, 3.0, ((0, 4),), jnp.float32),
    }


def dequantize(mantissa, exponent):
    scales = jnp.exp2(exponent.astype(jnp.float32))
    blocks = mantissa.astype(jnp.float32).reshape(D // BLK, BLK, F // BLK, BLK)
    return (blocks * scales[:, None, :, None]).reshape(D, F).astype(jnp.bfloat16)


def reference(resid_stream, enc_mantissa, enc_exponent, enc_bias, dec_weight, dec_bias):
    latents = []
    for layer_index in range(LAYERS):
        weight = dequantize(enc_mantissa[layer_index], enc_exponent[layer_index])
        pre_act = jnp.dot(resid_stream[:, layer_index, :], weight, preferred_element_type=jnp.float32)
        latents.append(jnp.maximum(pre_act + enc_bias[layer_index][None, :], 0.0).astype(jnp.bfloat16))
    outputs = []
    for target in range(LAYERS):
        total = jnp.zeros((TOKENS, D), jnp.float32)
        for source in range(target + 1):
            pair_index = target * (target + 1) // 2 + source
            total = total + jnp.dot(latents[source], dec_weight[pair_index], preferred_element_type=jnp.float32)
        outputs.append((total + dec_bias[target][None, :]).astype(jnp.bfloat16))
    return jnp.stack(outputs, axis=1)
```

```python
import jax
import jax.numpy as jnp
from jax import lax
from jax.experimental import pallas as pl
from jax.experimental.pallas import tpu as pltpu
from jax.sharding import PartitionSpec as P

BLK = 128
VMEM = pl.BlockSpec(memory_space=pltpu.VMEM)
LIMIT = 12 * 1024 * 1024


def encode_kernel(x_ref, mantissa_ref, exponent_ref, bias_ref, latent_ref):
    x = x_ref[...].astype(jnp.float32)
    tokens, width = x.shape
    features = mantissa_ref.shape[1]
    rows, blocks = exponent_ref.shape
    scale = jnp.exp2(exponent_ref[...].astype(jnp.float32)).astype(jnp.bfloat16)
    row_of = lax.broadcasted_iota(jnp.int32, (rows, width), 1) // BLK
    spread = (row_of == lax.broadcasted_iota(jnp.int32, (rows, width), 0)).astype(jnp.bfloat16)
    scales = lax.dot_general(scale, spread, (((0,), (0,)), ((), ())), preferred_element_type=jnp.float32)
    for first in range(0, blocks, 2):
        group = range(first, min(first + 2, blocks))
        scaled = jnp.concatenate([x * scales[j : j + 1, :] for j in group], axis=0).astype(jnp.bfloat16)
        columns = slice(first * BLK, (first + len(group)) * BLK)
        product = jnp.dot(scaled, mantissa_ref[:, columns], preferred_element_type=jnp.float32)
        for at, j in enumerate(group):
            own = product[at * tokens : (at + 1) * tokens, at * BLK : (at + 1) * BLK]
            there = slice(j * BLK, (j + 1) * BLK)
            latent_ref[:, there] = jnp.maximum(own + bias_ref[:, there], 0.0).astype(latent_ref.dtype)


def decode_kernel(latent_ref, weight_ref, out_ref):
    layers, tokens, _ = latent_ref.shape
    for target in range(layers):
        total = None
        for source in range(target + 1):
            pair = target * (target + 1) // 2 + source
            part = lax.dot_general(
                latent_ref[source],
                weight_ref[pair],
                (((1,), (1,)), ((), ())),
                preferred_element_type=jnp.float32,
            )
            total = part if total is None else total + part
        for token in range(tokens):
            out_ref[target * tokens + token] = total[token : token + 1, :]


def finish_kernel(parts_ref, bias_ref, out_ref):
    layers, shards, columns = parts_ref.shape[0], parts_ref.shape[1], parts_ref.shape[3]
    for block in range(layers):
        there = slice(block * columns, (block + 1) * columns)
        total = parts_ref[block, 0]
        for shard in range(1, shards):
            total = total + parts_ref[block, shard]
        out_ref[:, 0, there] = (total + bias_ref[:, there]).astype(out_ref.dtype)


def shards(resid_stream, enc_mantissa, enc_exponent, enc_bias, dec_weight, dec_bias):
    layer_count, feat_count = lax.axis_size("layer"), lax.axis_size("feat")
    tok_local, _, width = resid_stream.shape
    tokens = tok_local * feat_count
    feat_local = enc_mantissa.shape[2]
    col_local = dec_weight.shape[2]
    params = pltpu.CompilerParams(vmem_limit_bytes=LIMIT)

    spread = jnp.broadcast_to(resid_stream, (feat_count, tok_local, 1, width)).reshape(tokens, 1, width)
    x = lax.all_to_all(spread, "feat", 0, 0, tiled=True).reshape(tokens, width)
    latent = pl.pallas_call(
        encode_kernel,
        out_shape=jax.ShapeDtypeStruct((tokens, feat_local), jnp.bfloat16),
        in_specs=[VMEM] * 4,
        out_specs=VMEM,
        compiler_params=params,
        name="encode",
    )(x, enc_mantissa[0], enc_exponent[0], enc_bias)
    stacked = lax.all_gather(latent[None], "layer", axis=0, tiled=True)
    parts = pl.pallas_call(
        decode_kernel,
        out_shape=jax.ShapeDtypeStruct((layer_count * tokens, 1, col_local), jnp.float32),
        in_specs=[VMEM] * 2,
        out_specs=VMEM,
        compiler_params=params,
        name="decode",
    )(stacked, jnp.swapaxes(dec_weight, 1, 2))
    arrived = lax.all_to_all(parts, ("layer", "feat"), 0, 0, tiled=True)
    return pl.pallas_call(
        finish_kernel,
        out_shape=jax.ShapeDtypeStruct((tok_local, 1, width), jnp.bfloat16),
        in_specs=[VMEM] * 2,
        out_specs=VMEM,
        compiler_params=params,
        name="finish",
    )(arrived.reshape(layer_count, feat_count, tok_local, col_local), dec_bias)


def solution(mesh):
    in_specs = (
        P("feat", "layer", None),
        P("layer", None, "feat"),
        P("layer", None, "feat"),
        P("layer", "feat"),
        P(None, "feat", "layer"),
        P("layer", None),
    )
    out_specs = P("feat", "layer", None)
    return jax.shard_map(shards, mesh=mesh, in_specs=in_specs, out_specs=out_specs, check_vma=False)
```

```python
import jax
import jax.numpy as jnp
from jax import lax
from jax.experimental import pallas as pl
from jax.experimental.pallas import tpu as pltpu
from jax.sharding import PartitionSpec as P

BLK = 128
AXES = ("layer", "feat")
VMEM = pl.BlockSpec(memory_space=pltpu.VMEM)
LIMIT = 8 * 1024 * 1024
WORK = 20_000_000_000
OVER_ROWS = (((1,), (1,)), ((), ()))


def cost(flops):
    return pl.CostEstimate(flops=flops, bytes_accessed=0, transcendentals=0)


def prepare_kernel(own_ref, copies_ref):
    own = own_ref[0].astype(jnp.float32)
    for copy in range(copies_ref.shape[0]):
        copies_ref[copy] = own


def encode_kernel(all_ref, mantissa_ref, exponent_ref, bias_ref, latent_ref):
    x = all_ref[:, 0, :]
    tokens, width = x.shape
    blocks, rows = exponent_ref.shape
    scale = jnp.exp2(exponent_ref[...].astype(jnp.float32)).astype(jnp.bfloat16)
    row_of = lax.broadcasted_iota(jnp.int32, (rows, width), 1) // BLK
    spread = (row_of == lax.broadcasted_iota(jnp.int32, (rows, width), 0)).astype(jnp.bfloat16)
    scales = jnp.dot(scale, spread, preferred_element_type=jnp.float32)
    for first in range(0, blocks, 2):
        group = range(first, min(first + 2, blocks))
        scaled = jnp.concatenate([x * scales[j : j + 1, :] for j in group], axis=0).astype(jnp.bfloat16)
        columns = slice(first * BLK, (first + len(group)) * BLK)
        product = jnp.dot(scaled, mantissa_ref[:, columns], preferred_element_type=jnp.float32)
        for at, j in enumerate(group):
            own = product[at * tokens : (at + 1) * tokens, at * BLK : (at + 1) * BLK]
            there = slice(j * BLK, (j + 1) * BLK)
            latent_ref[:, there] = jnp.maximum(own + bias_ref[:, there], 0.0).astype(latent_ref.dtype)


def decode_kernel(near_ref, far_ref, weight_ref, out_ref):
    layer, shard = lax.axis_index("layer"), lax.axis_index("feat")
    half, tokens, _ = near_ref.shape
    layers = 2 * half
    out_rows = out_ref.shape[0] // layers
    latents = []
    for source in range(layers):
        slot = layer ^ source
        latents.append(jnp.where(slot < half, near_ref[slot % half], far_ref[slot % half]))
    for target in range(layers):
        total = None
        for source in range(target + 1):
            pair = target * (target + 1) // 2 + source
            part = lax.dot_general(latents[source], weight_ref[pair], OVER_ROWS, preferred_element_type=jnp.float32)
            total = part if total is None else total + part
        for token in range(tokens):
            out_ref[target * out_rows + token] = total[token : token + 1, :]


def finish_kernel(parts_ref, bias_ref, out_ref):
    layers, shards, columns = parts_ref.shape[0], parts_ref.shape[1], parts_ref.shape[3]
    for block in range(layers):
        there = slice(block * columns, (block + 1) * columns)
        total = parts_ref[block, 0]
        for shard in range(1, shards):
            total = total + parts_ref[block, shard]
        out_ref[:, 0, there] = (total + bias_ref[:, there]).astype(out_ref.dtype)


def shards(resid_stream, enc_mantissa, enc_exponent, enc_bias, dec_weight, dec_bias):
    layer_count, feat_count = lax.axis_size("layer"), lax.axis_size("feat")
    tok_local, _, width = resid_stream.shape
    tokens = tok_local * feat_count
    feat_local = enc_mantissa.shape[2]
    col_local = dec_weight.shape[2]
    params = pltpu.CompilerParams(vmem_limit_bytes=LIMIT)

    def place(layer, feat):
        return layer * feat_count + feat

    everywhere = [(layer, feat) for layer in range(layer_count) for feat in range(feat_count)]

    def swap(array, layer_bit=0, feat_bit=0, parities=(0, 1)):
        return lax.ppermute(
            array,
            AXES,
            [(place(l, f), place(l ^ layer_bit, f ^ feat_bit)) for l, f in everywhere if l % 2 in parities],
        )

    copies = pl.pallas_call(
        prepare_kernel,
        out_shape=jax.ShapeDtypeStruct((tokens, 1, width), jnp.float32),
        in_specs=[VMEM],
        out_specs=VMEM,
        compiler_params=params,
        cost_estimate=cost(WORK),
        name="prepare",
    )(resid_stream)
    gathered = lax.all_to_all(copies, "feat", 0, 0, tiled=True)
    latent = pl.pallas_call(
        encode_kernel,
        out_shape=jax.ShapeDtypeStruct((tokens, feat_local), jnp.bfloat16),
        in_specs=[VMEM] * 4,
        out_specs=VMEM,
        compiler_params=params,
        cost_estimate=cost(WORK),
        name="encode",
    )(gathered, enc_mantissa[0], jnp.swapaxes(enc_exponent[0], 0, 1), enc_bias)
    near = jnp.stack([latent, swap(latent, layer_bit=1)])
    far = swap(near, layer_bit=2)
    parts = pl.pallas_call(
        decode_kernel,
        out_shape=jax.ShapeDtypeStruct((layer_count * tokens, 1, col_local), jnp.float32),
        in_specs=[VMEM] * 3,
        out_specs=VMEM,
        compiler_params=params,
        cost_estimate=cost(WORK),
        name="decode",
    )(near, far, jnp.swapaxes(dec_weight, 1, 2))
    arrived = lax.all_to_all(parts, AXES, 0, 0, tiled=True)
    return pl.pallas_call(
        finish_kernel,
        out_shape=jax.ShapeDtypeStruct((tok_local, 1, width), jnp.bfloat16),
        in_specs=[VMEM] * 2,
        out_specs=VMEM,
        compiler_params=params,
        name="finish",
    )(arrived.reshape(layer_count, feat_count, tok_local, col_local), dec_bias)


def solution(mesh):
    in_specs = (
        P("feat", "layer", None),
        P("layer", None, "feat"),
        P("layer", None, "feat"),
        P("layer", "feat"),
        P(None, "feat", "layer"),
        P("layer", None),
    )
    out_specs = P("feat", "layer", None)
    return jax.shard_map(shards, mesh=mesh, in_specs=in_specs, out_specs=out_specs, check_vma=False)
```

```python
import functools

import jax
import jax.numpy as jnp
from jax import lax
from jax.experimental import pallas as pl
from jax.experimental.pallas import tpu as pltpu
from jax.sharding import PartitionSpec as P

BLK = 128
AXES = ("layer", "feat")
VMEM = pl.BlockSpec(memory_space=pltpu.VMEM)
LIMIT = 8 * 1024 * 1024
WORK = 20_000_000_000
OVER_ROWS = (((1,), (1,)), ((), ()))


def kernel(body, out_shape, name, scratch_shapes=()):
    def call(*operands):
        return pl.pallas_call(
            body,
            out_shape=out_shape,
            in_specs=[VMEM] * len(operands),
            out_specs=VMEM,
            scratch_shapes=scratch_shapes,
            compiler_params=pltpu.CompilerParams(vmem_limit_bytes=LIMIT),
            cost_estimate=pl.CostEstimate(flops=WORK, bytes_accessed=0, transcendentals=0),
            name=name,
        )(*operands)

    return call


def prepare_kernel(own_ref, copies_ref):
    own = own_ref[0].astype(jnp.float32)
    for copy in range(copies_ref.shape[0]):
        copies_ref[copy] = own


def encode_kernel(all_ref, mantissa_ref, exponent_ref, bias_ref, latent_ref):
    x = all_ref[:, 0, :]
    tokens, width = x.shape
    blocks, rows = exponent_ref.shape
    scale = jnp.exp2(exponent_ref[...].astype(jnp.float32)).astype(jnp.bfloat16)
    row_of = lax.broadcasted_iota(jnp.int32, (rows, width), 1) // BLK
    spread = (row_of == lax.broadcasted_iota(jnp.int32, (rows, width), 0)).astype(jnp.bfloat16)
    scales = jnp.dot(scale, spread, preferred_element_type=jnp.float32)
    for first in range(0, blocks, 2):
        group = range(first, min(first + 2, blocks))
        scaled = jnp.concatenate([x * scales[j : j + 1, :] for j in group], axis=0).astype(jnp.bfloat16)
        columns = slice(first * BLK, (first + len(group)) * BLK)
        product = jnp.dot(scaled, mantissa_ref[:, columns], preferred_element_type=jnp.float32)
        for at, j in enumerate(group):
            own = product[at * tokens : (at + 1) * tokens, at * BLK : (at + 1) * BLK]
            there = slice(j * BLK, (j + 1) * BLK)
            latent_ref[:, there] = jnp.maximum(own + bias_ref[:, there], 0.0).astype(latent_ref.dtype)


def product(latent, weight_ref, pair):
    columns, features = weight_ref.shape[1:]
    still, step = columns // 512 * 256, min(features, 256)
    fixed, moved = None, None
    for at in range(0, features, step):
        there = slice(at, at + step)
        if still:
            part = lax.dot_general(
                latent[:, there], weight_ref[pair, :still, there], OVER_ROWS, preferred_element_type=jnp.float32
            )
            fixed = part if fixed is None else fixed + part
        part = lax.dot_general(
            weight_ref[pair, still:, there], latent[:, there], OVER_ROWS, preferred_element_type=jnp.float32
        )
        moved = part if moved is None else moved + part
    return jnp.concatenate([fixed, moved.T], axis=1) if still else moved.T


def add_pair(total_ref, latent, weight_ref, source, target):
    total_ref[target] += product(latent, weight_ref, target * (target + 1) // 2 + source)


def decode_own_kernel(own_ref, weight_ref, total_ref):
    layer, layers = lax.axis_index("layer"), total_ref.shape[0]
    total_ref[...] = jnp.zeros_like(total_ref)

    count = layers - layer

    @pl.when(count % 2 == 1)
    def _():
        add_pair(total_ref, own_ref[...], weight_ref, layer, layer)

    for first in range(0, layers, 2):

        @pl.when(first + 2 <= count)
        def _():
            for at in (first, first + 1):
                add_pair(total_ref, own_ref[...], weight_ref, layer, layer + count % 2 + at)


def decode_far_kernel(parity, total_ref, far_ref, weight_ref, out_ref):
    layer, layers = lax.axis_index("layer"), total_ref.shape[0]
    out_ref[...] = total_ref[...]
    source = layer ^ 2
    count = jnp.where(layer % 2 == parity, layers - source, 0)

    @pl.when(count % 2 == 1)
    def _():
        add_pair(out_ref, far_ref[...], weight_ref, source, source)

    for first in range(0, layers, 2):

        @pl.when(first + 2 <= count)
        def _():
            for at in (first, first + 1):
                add_pair(out_ref, far_ref[...], weight_ref, source, source + count % 2 + at)


def decode_last_kernel(total_ref, both_ref, weight_ref, out_ref, sum_ref):
    layer, layers = lax.axis_index("layer"), total_ref.shape[0]
    tokens = both_ref.shape[1]
    sum_ref[...] = total_ref[...]
    sources = (layer ^ 1, layer ^ 3)
    first_count = layers - sources[0]
    count = first_count + layers - sources[1]

    def step(at):
        at_first = at < first_count
        source = jnp.where(at_first, sources[0], sources[1])
        target = jnp.where(at_first, sources[0] + at, sources[1] + at - first_count)
        add_pair(sum_ref, both_ref[jnp.where(at_first, 0, 1)], weight_ref, source, target)

    for at in range(layers):
        step(at)

    @pl.when(count > layers)
    def _():
        for at in (layers, layers + 1):
            step(at)

    for target in range(layers):
        total = sum_ref[target]
        for token in range(tokens):
            out_ref[target * tokens + token] = total[token : token + 1, :]


def finish_kernel(parts_ref, bias_ref, out_ref):
    layers, shards, columns = parts_ref.shape[0], parts_ref.shape[1], parts_ref.shape[3]
    for block in range(layers):
        there = slice(block * columns, (block + 1) * columns)
        total = parts_ref[block, 0]
        for shard in range(1, shards):
            total = total + parts_ref[block, shard]
        out_ref[:, 0, there] = (total + bias_ref[:, there]).astype(out_ref.dtype)


def shards(resid_stream, enc_mantissa, enc_exponent, enc_bias, dec_weight, dec_bias):
    layer_count, feat_count = lax.axis_size("layer"), lax.axis_size("feat")
    tok_local, _, width = resid_stream.shape
    tokens = tok_local * feat_count
    feat_local = enc_mantissa.shape[2]
    col_local = dec_weight.shape[2]

    def place(layer, feat):
        return layer * feat_count + feat

    everywhere = [(layer, feat) for layer in range(layer_count) for feat in range(feat_count)]

    def swap(array, layer_bit=0, feat_bit=0, parities=(0, 1)):
        return lax.ppermute(
            array,
            AXES,
            [(place(l, f), place(l ^ layer_bit, f ^ feat_bit)) for l, f in everywhere if l % 2 in parities],
        )

    copies = kernel(prepare_kernel, jax.ShapeDtypeStruct((tokens, 1, width), jnp.float32), "prepare")(resid_stream)
    gathered = lax.all_to_all(copies, "feat", 0, 0, tiled=True)
    latent = kernel(encode_kernel, jax.ShapeDtypeStruct((tokens, feat_local), jnp.bfloat16), "encode")(
        gathered, enc_mantissa[0], jnp.swapaxes(enc_exponent[0], 0, 1), enc_bias
    )
    weight = jnp.swapaxes(dec_weight, 1, 2)
    total = jax.ShapeDtypeStruct((layer_count, tokens, col_local), jnp.float32)
    far = swap(latent, layer_bit=2)
    own_total = kernel(decode_own_kernel, total, "decode_own")(latent, weight)
    odd_total = kernel(functools.partial(decode_far_kernel, 1), total, "decode_far_odd")(own_total, far, weight)
    held, odd_total = lax.optimization_barrier((jnp.stack([latent, far]), odd_total))
    both = swap(held, layer_bit=1)
    even_total = kernel(functools.partial(decode_far_kernel, 0), total, "decode_far_even")(odd_total, far, weight)
    parts = kernel(
        decode_last_kernel,
        jax.ShapeDtypeStruct((layer_count * tokens, 1, col_local), jnp.float32),
        "decode_last",
        scratch_shapes=[pltpu.VMEM(total.shape, total.dtype)],
    )(even_total, both, weight)
    arrived = lax.all_to_all(parts, AXES, 0, 0, tiled=True)
    return kernel(finish_kernel, jax.ShapeDtypeStruct((tok_local, 1, width), jnp.bfloat16), "finish")(
        arrived.reshape(layer_count, feat_count, tok_local, col_local), dec_bias
    )


def solution(mesh):
    in_specs = (
        P("feat", "layer", None),
        P("layer", None, "feat"),
        P("layer", None, "feat"),
        P("layer", "feat"),
        P(None, "feat", "layer"),
        P("layer", None),
    )
    out_specs = P("feat", "layer", None)
    return jax.shard_map(shards, mesh=mesh, in_specs=in_specs, out_specs=out_specs, check_vma=False)
```

```python
import functools

import jax
import jax.numpy as jnp
from jax import lax
from jax.experimental import pallas as pl
from jax.experimental.pallas import tpu as pltpu
from jax.sharding import PartitionSpec as P

BLK = 128
AXES = ("layer", "feat")
VMEM = pl.BlockSpec(memory_space=pltpu.VMEM)
LIMIT = 8 * 1024 * 1024
WORK = 20_000_000_000
OVER_ROWS = (((1,), (1,)), ((), ()))


def kernel(body, out_shape, name, scratch_shapes=()):
    def call(*operands):
        return pl.pallas_call(
            body,
            out_shape=out_shape,
            in_specs=[VMEM] * len(operands),
            out_specs=VMEM,
            scratch_shapes=scratch_shapes,
            compiler_params=pltpu.CompilerParams(vmem_limit_bytes=LIMIT),
            cost_estimate=pl.CostEstimate(flops=WORK, bytes_accessed=0, transcendentals=0),
            name=name,
        )(*operands)

    return call


def prepare_kernel(own_ref, copies_ref):
    own = own_ref[0].astype(jnp.float32)
    for copy in range(copies_ref.shape[0]):
        copies_ref[copy] = own


def encode_kernel(all_ref, mantissa_ref, exponent_ref, bias_ref, latent_ref):
    x = all_ref[:, 0, :]
    tokens, width = x.shape
    blocks, rows = exponent_ref.shape
    scale = jnp.exp2(exponent_ref[...].astype(jnp.float32)).astype(jnp.bfloat16)
    row_of = lax.broadcasted_iota(jnp.int32, (rows, width), 1) // BLK
    spread = (row_of == lax.broadcasted_iota(jnp.int32, (rows, width), 0)).astype(jnp.bfloat16)
    scales = jnp.dot(scale, spread, preferred_element_type=jnp.float32)
    for first in range(0, blocks, 2):
        group = range(first, min(first + 2, blocks))
        scaled = jnp.concatenate([x * scales[j : j + 1, :] for j in group], axis=0).astype(jnp.bfloat16)
        columns = slice(first * BLK, (first + len(group)) * BLK)
        product = jnp.dot(scaled, mantissa_ref[:, columns], preferred_element_type=jnp.float32)
        for at, j in enumerate(group):
            own = product[at * tokens : (at + 1) * tokens, at * BLK : (at + 1) * BLK]
            there = slice(j * BLK, (j + 1) * BLK)
            latent_ref[:, there] = jnp.maximum(own + bias_ref[:, there], 0.0).astype(latent_ref.dtype)


def products(latents, weight_ref, target):
    columns, features = weight_ref.shape[1:]
    still, step = columns // 512 * 256, min(features, 256)
    fixed, moved = None, None
    for source, latent in latents:
        pair = target * (target + 1) // 2 + source
        for at in range(0, features, step):
            there = slice(at, at + step)
            if still:
                part = lax.dot_general(
                    latent[:, there], weight_ref[pair, :still, there], OVER_ROWS, preferred_element_type=jnp.float32
                )
                fixed = part if fixed is None else fixed + part
            part = lax.dot_general(
                weight_ref[pair, still:, there], latent[:, there], OVER_ROWS, preferred_element_type=jnp.float32
            )
            moved = part if moved is None else moved + part
    return jnp.concatenate([fixed, moved.T], axis=1) if still else moved.T


def on_each_layer(layers, body):
    for layer in range(layers):

        @pl.when(lax.axis_index("layer") == layer)
        def _():
            body(layer)


def decode_own_kernel(own_ref, weight_ref, total_ref):
    layers = total_ref.shape[0]

    def body(layer):
        for target in range(layers):
            if layer <= target:
                total_ref[target] = products([(layer, own_ref[...])], weight_ref, target)
            else:
                total_ref[target] = jnp.zeros(total_ref.shape[1:], total_ref.dtype)

    on_each_layer(layers, body)


def decode_more_kernel(offset, total_ref, latent_ref, weight_ref, out_ref):
    layers = total_ref.shape[0]

    def body(layer):
        source = layer ^ offset
        for target in range(layers):
            total = total_ref[target]
            if source <= target:
                total = total + products([(source, latent_ref[...])], weight_ref, target)
            out_ref[target] = total

    on_each_layer(layers, body)


def decode_last_kernel(total_ref, last_ref, weight_ref, out_ref):
    layers, tokens, _ = total_ref.shape

    def body(layer):
        source = layer ^ 3
        for target in range(layers):
            total = total_ref[target]
            if source <= target:
                total = total + products([(source, last_ref[...])], weight_ref, target)
            for token in range(tokens):
                out_ref[target * tokens + token] = total[token : token + 1, :]

    on_each_layer(layers, body)


def finish_kernel(parts_ref, bias_ref, out_ref):
    layers, shards, columns = parts_ref.shape[0], parts_ref.shape[1], parts_ref.shape[3]
    for block in range(layers):
        there = slice(block * columns, (block + 1) * columns)
        total = parts_ref[block, 0]
        for shard in range(1, shards):
            total = total + parts_ref[block, shard]
        out_ref[:, 0, there] = (total + bias_ref[:, there]).astype(out_ref.dtype)


def shards(resid_stream, enc_mantissa, enc_exponent, enc_bias, dec_weight, dec_bias):
    layer_count, feat_count = lax.axis_size("layer"), lax.axis_size("feat")
    tok_local, _, width = resid_stream.shape
    tokens = tok_local * feat_count
    feat_local = enc_mantissa.shape[2]
    col_local = dec_weight.shape[2]

    def place(layer, feat):
        return layer * feat_count + feat

    everywhere = [(layer, feat) for layer in range(layer_count) for feat in range(feat_count)]

    def swap(array, layer_bit=0, feat_bit=0, parities=(0, 1)):
        return lax.ppermute(
            array,
            AXES,
            [(place(l, f), place(l ^ layer_bit, f ^ feat_bit)) for l, f in everywhere if l % 2 in parities],
        )

    copies = kernel(prepare_kernel, jax.ShapeDtypeStruct((tokens, 1, width), jnp.float32), "prepare")(resid_stream)
    gathered = lax.all_to_all(copies, "feat", 0, 0, tiled=True)
    latent = kernel(encode_kernel, jax.ShapeDtypeStruct((tokens, feat_local), jnp.bfloat16), "encode")(
        gathered, enc_mantissa[0], jnp.swapaxes(enc_exponent[0], 0, 1), enc_bias
    )
    weight = jnp.swapaxes(dec_weight, 1, 2)
    total = jax.ShapeDtypeStruct((layer_count, tokens, col_local), jnp.float32)
    far = swap(latent, layer_bit=2)
    core = swap(latent, layer_bit=1)
    own_total = kernel(decode_own_kernel, total, "decode_own")(latent, weight)
    chip_total = kernel(functools.partial(decode_more_kernel, 1), total, "decode_core")(own_total, core, weight)
    far, chip_total = lax.optimization_barrier((far, chip_total))
    last = swap(far, layer_bit=1)
    far_total = kernel(functools.partial(decode_more_kernel, 2), total, "decode_far")(chip_total, far, weight)
    parts = kernel(
        decode_last_kernel, jax.ShapeDtypeStruct((layer_count * tokens, 1, col_local), jnp.float32), "decode_last"
    )(far_total, last, weight)
    arrived = lax.all_to_all(parts, AXES, 0, 0, tiled=True)
    return kernel(finish_kernel, jax.ShapeDtypeStruct((tok_local, 1, width), jnp.bfloat16), "finish")(
        arrived.reshape(layer_count, feat_count, tok_local, col_local), dec_bias
    )


def solution(mesh):
    in_specs = (
        P("feat", "layer", None),
        P("layer", None, "feat"),
        P("layer", None, "feat"),
        P("layer", "feat"),
        P(None, "feat", "layer"),
        P("layer", None),
    )
    out_specs = P("feat", "layer", None)
    return jax.shard_map(shards, mesh=mesh, in_specs=in_specs, out_specs=out_specs, check_vma=False)
```

```python
import functools

import jax
import jax.numpy as jnp
from jax import lax
from jax.experimental import pallas as pl
from jax.experimental.pallas import tpu as pltpu
from jax.sharding import PartitionSpec as P

BLK = 128
AXES = ("layer", "feat")
VMEM = pl.BlockSpec(memory_space=pltpu.VMEM)
LIMIT = 8 * 1024 * 1024
WORK = 2_000_000_000
OVER_ROWS = (((1,), (1,)), ((), ()))


def kernel(body, out_shape, name, scratch_shapes=(), work=WORK):
    def call(*operands):
        return pl.pallas_call(
            body,
            out_shape=out_shape,
            in_specs=[VMEM] * len(operands),
            out_specs=VMEM,
            scratch_shapes=scratch_shapes,
            compiler_params=pltpu.CompilerParams(vmem_limit_bytes=LIMIT),
            cost_estimate=pl.CostEstimate(flops=work, bytes_accessed=0, transcendentals=0),
            name=name,
        )(*operands)

    return call


def prepare_kernel(own_ref, copies_ref):
    own = own_ref[0].astype(jnp.float32)
    for copy in range(copies_ref.shape[0]):
        copies_ref[copy] = own


def encode_kernel(all_ref, mantissa_ref, exponent_ref, bias_ref, latent_ref):
    x = all_ref[:, 0, :]
    tokens, width = x.shape
    blocks, rows = exponent_ref.shape
    scale = jnp.exp2(exponent_ref[...].astype(jnp.float32)).astype(jnp.bfloat16)
    row_of = lax.broadcasted_iota(jnp.int32, (rows, width), 1) // BLK
    spread = (row_of == lax.broadcasted_iota(jnp.int32, (rows, width), 0)).astype(jnp.bfloat16)
    scales = jnp.dot(scale, spread, preferred_element_type=jnp.float32)
    for first in range(0, blocks, 2):
        group = range(first, min(first + 2, blocks))
        scaled = jnp.concatenate([x * scales[j : j + 1, :] for j in group], axis=0).astype(jnp.bfloat16)
        columns = slice(first * BLK, (first + len(group)) * BLK)
        product = jnp.dot(scaled, mantissa_ref[:, columns], preferred_element_type=jnp.float32)
        for at, j in enumerate(group):
            own = product[at * tokens : (at + 1) * tokens, at * BLK : (at + 1) * BLK]
            there = slice(j * BLK, (j + 1) * BLK)
            latent_ref[:, there] = jnp.maximum(own + bias_ref[:, there], 0.0).astype(latent_ref.dtype)


def products(latents, weight_ref, target):
    columns, features = weight_ref.shape[1:]
    still, step = columns // 512 * 256, min(features, 256)
    fixed, moved = None, None
    for source, latent in latents:
        pair = target * (target + 1) // 2 + source
        for at in range(0, features, step):
            there = slice(at, at + step)
            if still:
                part = lax.dot_general(
                    latent[:, there], weight_ref[pair, :still, there], OVER_ROWS, preferred_element_type=jnp.float32
                )
                fixed = part if fixed is None else fixed + part
            part = lax.dot_general(
                weight_ref[pair, still:, there], latent[:, there], OVER_ROWS, preferred_element_type=jnp.float32
            )
            moved = part if moved is None else moved + part
    return jnp.concatenate([fixed, moved.T], axis=1) if still else moved.T


def on_each_layer(layers, body):
    for layer in range(layers):

        @pl.when(lax.axis_index("layer") == layer)
        def _():
            body(layer)


def decode_own_kernel(own_ref, weight_ref, total_ref):
    layers = total_ref.shape[0]

    def body(layer):
        for target in range(layers):
            if layer <= target:
                total_ref[target] = products([(layer, own_ref[...])], weight_ref, target)
            else:
                total_ref[target] = jnp.zeros(total_ref.shape[1:], total_ref.dtype)

    on_each_layer(layers, body)


def decode_more_kernel(offset, total_ref, latent_ref, weight_ref, out_ref):
    layers = total_ref.shape[0]

    def body(layer):
        source = layer ^ offset
        for target in range(layers):
            total = total_ref[target]
            if source <= target:
                total = total + products([(source, latent_ref[...])], weight_ref, target)
            out_ref[target] = total

    on_each_layer(layers, body)


def decode_last_kernel(total_ref, last_ref, weight_ref, out_ref):
    layers, tokens, _ = total_ref.shape

    def body(layer):
        source = layer ^ 2
        for target in range(layers):
            total = total_ref[target]
            if source <= target:
                total = total + products([(source, last_ref[...])], weight_ref, target)
            for token in range(tokens):
                out_ref[target * tokens + token] = total[token : token + 1, :]

    on_each_layer(layers, body)


def finish_kernel(parts_ref, bias_ref, out_ref):
    layers, shards, columns = parts_ref.shape[0], parts_ref.shape[1], parts_ref.shape[3]
    for block in range(layers):
        there = slice(block * columns, (block + 1) * columns)
        total = parts_ref[block, 0]
        for shard in range(1, shards):
            total = total + parts_ref[block, shard]
        out_ref[:, 0, there] = (total + bias_ref[:, there]).astype(out_ref.dtype)


def shards(resid_stream, enc_mantissa, enc_exponent, enc_bias, dec_weight, dec_bias):
    layer_count, feat_count = lax.axis_size("layer"), lax.axis_size("feat")
    tok_local, _, width = resid_stream.shape
    tokens = tok_local * feat_count
    feat_local = enc_mantissa.shape[2]
    col_local = dec_weight.shape[2]

    def place(layer, feat):
        return layer * feat_count + feat

    everywhere = [(layer, feat) for layer in range(layer_count) for feat in range(feat_count)]

    def swap(array, layer_bit=0, feat_bit=0, parities=(0, 1)):
        return lax.ppermute(
            array,
            AXES,
            [(place(l, f), place(l ^ layer_bit, f ^ feat_bit)) for l, f in everywhere if l % 2 in parities],
        )

    copies = kernel(prepare_kernel, jax.ShapeDtypeStruct((tokens, 1, width), jnp.float32), "prepare", work=20 * WORK)(resid_stream)
    gathered = lax.all_to_all(copies, "feat", 0, 0, tiled=True)
    latent = kernel(encode_kernel, jax.ShapeDtypeStruct((tokens, feat_local), jnp.bfloat16), "encode")(
        gathered, enc_mantissa[0], jnp.swapaxes(enc_exponent[0], 0, 1), enc_bias
    )
    weight = jnp.swapaxes(dec_weight, 1, 2)
    total = jax.ShapeDtypeStruct((layer_count, tokens, col_local), jnp.float32)
    far = swap(latent, layer_bit=3)
    core = swap(latent, layer_bit=1)
    own_total = kernel(decode_own_kernel, total, "decode_own")(latent, weight)
    chip_total = kernel(functools.partial(decode_more_kernel, 1), total, "decode_core")(own_total, core, weight)
    far, chip_total = lax.optimization_barrier((far, chip_total))
    last = swap(far, layer_bit=1)
    far_total = kernel(functools.partial(decode_more_kernel, 3), total, "decode_far")(chip_total, far, weight)
    parts = kernel(
        decode_last_kernel, jax.ShapeDtypeStruct((layer_count * tokens, 1, col_local), jnp.float32), "decode_last"
    )(far_total, last, weight)
    arrived = lax.all_to_all(parts, AXES, 0, 0, tiled=True)
    return kernel(finish_kernel, jax.ShapeDtypeStruct((tok_local, 1, width), jnp.bfloat16), "finish")(
        arrived.reshape(layer_count, feat_count, tok_local, col_local), dec_bias
    )


def solution(mesh):
    in_specs = (
        P("feat", "layer", None),
        P("layer", None, "feat"),
        P("layer", None, "feat"),
        P("layer", "feat"),
        P(None, "feat", "layer"),
        P("layer", None),
    )
    out_specs = P("feat", "layer", None)
    return jax.shard_map(shards, mesh=mesh, in_specs=in_specs, out_specs=out_specs, check_vma=False)
```

```python
import functools

import jax
import jax.numpy as jnp
from jax import lax
from jax.experimental import pallas as pl
from jax.experimental.pallas import tpu as pltpu
from jax.sharding import PartitionSpec as P

BLK = 128
AXES = ("layer", "feat")
VMEM = pl.BlockSpec(memory_space=pltpu.VMEM)
LIMIT = 8 * 1024 * 1024
WORK = 2_000_000_000
OVER_ROWS = (((1,), (1,)), ((), ()))


def kernel(body, out_shape, name, scratch_shapes=(), work=WORK):
    def call(*operands):
        return pl.pallas_call(
            body,
            out_shape=out_shape,
            in_specs=[VMEM] * len(operands),
            out_specs=VMEM,
            scratch_shapes=scratch_shapes,
            compiler_params=pltpu.CompilerParams(vmem_limit_bytes=LIMIT),
            cost_estimate=pl.CostEstimate(flops=work, bytes_accessed=0, transcendentals=0),
            name=name,
        )(*operands)

    return call


def prepare_kernel(own_ref, copies_ref):
    own = own_ref[0].astype(jnp.float32)
    for copy in range(copies_ref.shape[0]):
        copies_ref[copy] = own


def encode_kernel(all_ref, mantissa_ref, exponent_ref, bias_ref, latent_ref):
    x = all_ref[:, 0, :]
    tokens, width = x.shape
    blocks, rows = exponent_ref.shape
    scale = jnp.exp2(exponent_ref[...].astype(jnp.float32)).astype(jnp.bfloat16)
    row_of = lax.broadcasted_iota(jnp.int32, (rows, width), 1) // BLK
    spread = (row_of == lax.broadcasted_iota(jnp.int32, (rows, width), 0)).astype(jnp.bfloat16)
    scales = jnp.dot(scale, spread, preferred_element_type=jnp.float32)
    for first in range(0, blocks, 2):
        group = range(first, min(first + 2, blocks))
        scaled = jnp.concatenate([x * scales[j : j + 1, :] for j in group], axis=0).astype(jnp.bfloat16)
        columns = slice(first * BLK, (first + len(group)) * BLK)
        product = jnp.dot(scaled, mantissa_ref[:, columns], preferred_element_type=jnp.float32)
        for at, j in enumerate(group):
            own = product[at * tokens : (at + 1) * tokens, at * BLK : (at + 1) * BLK]
            there = slice(j * BLK, (j + 1) * BLK)
            latent_ref[:, there] = jnp.maximum(own + bias_ref[:, there], 0.0).astype(latent_ref.dtype)


def products(latents, weight_ref, target):
    columns, features = weight_ref.shape[1:]
    still, step = columns // 512 * 256, min(features, 256)
    fixed, moved = None, None
    for source, latent in latents:
        pair = target * (target + 1) // 2 + source
        for at in range(0, features, step):
            there = slice(at, at + step)
            if still:
                part = lax.dot_general(
                    latent[:, there], weight_ref[pair, :still, there], OVER_ROWS, preferred_element_type=jnp.float32
                )
                fixed = part if fixed is None else fixed + part
            part = lax.dot_general(
                weight_ref[pair, still:, there], latent[:, there], OVER_ROWS, preferred_element_type=jnp.float32
            )
            moved = part if moved is None else moved + part
    return jnp.concatenate([fixed, moved.T], axis=1) if still else moved.T


def on_each_layer(layers, body):
    for layer in range(layers):

        @pl.when(lax.axis_index("layer") == layer)
        def _():
            body(layer)


def decode_chip_kernel(own_ref, core_ref, weight_ref, total_ref):
    layers = total_ref.shape[0]

    def body(layer):
        latents = [(layer, own_ref[...]), (layer ^ 1, core_ref[...])]
        for target in range(layers):
            reached = [entry for entry in latents if entry[0] <= target]
            if reached:
                total_ref[target] = products(reached, weight_ref, target)
            else:
                total_ref[target] = jnp.zeros(total_ref.shape[1:], total_ref.dtype)

    on_each_layer(layers, body)


def decode_more_kernel(offset, total_ref, latent_ref, weight_ref, out_ref):
    layers = total_ref.shape[0]

    def body(layer):
        source = layer ^ offset
        for target in range(layers):
            total = total_ref[target]
            if source <= target:
                total = total + products([(source, latent_ref[...])], weight_ref, target)
            out_ref[target] = total

    on_each_layer(layers, body)


def decode_last_kernel(total_ref, last_ref, weight_ref, out_ref):
    layers, tokens, _ = total_ref.shape

    def body(layer):
        source = layer ^ 2
        for target in range(layers):
            total = total_ref[target]
            if source <= target:
                total = total + products([(source, last_ref[...])], weight_ref, target)
            for token in range(tokens):
                out_ref[target * tokens + token] = total[token : token + 1, :]

    on_each_layer(layers, body)


def finish_kernel(parts_ref, bias_ref, out_ref):
    layers, shards, columns = parts_ref.shape[0], parts_ref.shape[1], parts_ref.shape[3]
    for block in range(layers):
        there = slice(block * columns, (block + 1) * columns)
        total = parts_ref[block, 0]
        for shard in range(1, shards):
            total = total + parts_ref[block, shard]
        out_ref[:, 0, there] = (total + bias_ref[:, there]).astype(out_ref.dtype)


def shards(resid_stream, enc_mantissa, enc_exponent, enc_bias, dec_weight, dec_bias):
    layer_count, feat_count = lax.axis_size("layer"), lax.axis_size("feat")
    tok_local, _, width = resid_stream.shape
    tokens = tok_local * feat_count
    feat_local = enc_mantissa.shape[2]
    col_local = dec_weight.shape[2]

    def place(layer, feat):
        return layer * feat_count + feat

    everywhere = [(layer, feat) for layer in range(layer_count) for feat in range(feat_count)]

    def swap(array, layer_bit=0, feat_bit=0, parities=(0, 1)):
        return lax.ppermute(
            array,
            AXES,
            [(place(l, f), place(l ^ layer_bit, f ^ feat_bit)) for l, f in everywhere if l % 2 in parities],
        )

    copies = kernel(prepare_kernel, jax.ShapeDtypeStruct((tokens, 1, width), jnp.float32), "prepare", work=20 * WORK)(resid_stream)
    gathered = lax.all_to_all(copies, "feat", 0, 0, tiled=True)
    latent = kernel(encode_kernel, jax.ShapeDtypeStruct((tokens, feat_local), jnp.bfloat16), "encode")(
        gathered, enc_mantissa[0], jnp.swapaxes(enc_exponent[0], 0, 1), enc_bias
    )
    weight = jnp.swapaxes(dec_weight, 1, 2)
    total = jax.ShapeDtypeStruct((layer_count, tokens, col_local), jnp.float32)
    core = swap(latent, layer_bit=1)
    other = swap(latent, layer_bit=3)
    held, core = lax.optimization_barrier((latent, core))
    same = swap(held, layer_bit=2)
    chip_total = kernel(decode_chip_kernel, total, "decode_chip")(latent, core, weight)
    most_total = kernel(functools.partial(decode_more_kernel, 3), total, "decode_other")(chip_total, other, weight)
    parts = kernel(
        decode_last_kernel, jax.ShapeDtypeStruct((layer_count * tokens, 1, col_local), jnp.float32), "decode_same"
    )(most_total, same, weight)
    arrived = lax.all_to_all(parts, AXES, 0, 0, tiled=True)
    return kernel(finish_kernel, jax.ShapeDtypeStruct((tok_local, 1, width), jnp.bfloat16), "finish")(
        arrived.reshape(layer_count, feat_count, tok_local, col_local), dec_bias
    )


def solution(mesh):
    in_specs = (
        P("feat", "layer", None),
        P("layer", None, "feat"),
        P("layer", None, "feat"),
        P("layer", "feat"),
        P(None, "feat", "layer"),
        P("layer", None),
    )
    out_specs = P("feat", "layer", None)
    return jax.shard_map(shards, mesh=mesh, in_specs=in_specs, out_specs=out_specs, check_vma=False)
```

```python
import functools

import jax
import jax.numpy as jnp
from jax import lax
from jax.experimental import pallas as pl
from jax.experimental.pallas import tpu as pltpu
from jax.sharding import PartitionSpec as P

BLK = 128
AXES = ("layer", "feat")
VMEM = pl.BlockSpec(memory_space=pltpu.VMEM)
LIMIT = 8 * 1024 * 1024
WORK = 2_000_000_000
OVER_ROWS = (((1,), (1,)), ((), ()))


def kernel(body, out_shape, name, scratch_shapes=(), work=WORK):
    def call(*operands):
        return pl.pallas_call(
            body,
            out_shape=out_shape,
            in_specs=[VMEM] * len(operands),
            out_specs=VMEM,
            scratch_shapes=scratch_shapes,
            compiler_params=pltpu.CompilerParams(vmem_limit_bytes=LIMIT),
            cost_estimate=pl.CostEstimate(flops=work, bytes_accessed=0, transcendentals=0),
            name=name,
        )(*operands)

    return call


def prepare_kernel(own_ref, copies_ref):
    _, parts, columns = copies_ref.shape
    own = own_ref[0].astype(jnp.float32)
    rows = [own[:, part * columns : (part + 1) * columns] for part in range(parts)]
    own = jnp.concatenate(rows, axis=0).astype(copies_ref.dtype)
    for copy in range(copies_ref.shape[0]):
        copies_ref[copy] = own


def encode_kernel(all_ref, mantissa_ref, exponent_ref, bias_ref, latent_ref):
    parts = all_ref[...].astype(jnp.float32)
    x = jnp.concatenate([parts[:, part, :] for part in range(parts.shape[1])], axis=1)
    tokens, width = x.shape
    blocks, rows = exponent_ref.shape
    scale = jnp.exp2(exponent_ref[...].astype(jnp.float32)).astype(jnp.bfloat16)
    row_of = lax.broadcasted_iota(jnp.int32, (rows, width), 1) // BLK
    spread = (row_of == lax.broadcasted_iota(jnp.int32, (rows, width), 0)).astype(jnp.bfloat16)
    scales = jnp.dot(scale, spread, preferred_element_type=jnp.float32)
    for first in range(0, blocks, 2):
        group = range(first, min(first + 2, blocks))
        scaled = jnp.concatenate([x * scales[j : j + 1, :] for j in group], axis=0).astype(jnp.bfloat16)
        columns = slice(first * BLK, (first + len(group)) * BLK)
        product = jnp.dot(scaled, mantissa_ref[:, columns], preferred_element_type=jnp.float32)
        for at, j in enumerate(group):
            own = product[at * tokens : (at + 1) * tokens, at * BLK : (at + 1) * BLK]
            there = slice(j * BLK, (j + 1) * BLK)
            latent_ref[:, there] = jnp.maximum(own + bias_ref[:, there], 0.0).astype(latent_ref.dtype)


def products(latents, weight_ref, target):
    columns, features = weight_ref.shape[1:]
    still, step = columns // 512 * 256, min(features, 256)
    fixed, moved = None, None
    for source, latent in latents:
        pair = target * (target + 1) // 2 + source
        for at in range(0, features, step):
            there = slice(at, at + step)
            if still:
                part = lax.dot_general(
                    latent[:, there], weight_ref[pair, :still, there], OVER_ROWS, preferred_element_type=jnp.float32
                )
                fixed = part if fixed is None else fixed + part
            part = lax.dot_general(
                weight_ref[pair, still:, there], latent[:, there], OVER_ROWS, preferred_element_type=jnp.float32
            )
            moved = part if moved is None else moved + part
    return jnp.concatenate([fixed, moved.T], axis=1) if still else moved.T


def on_each_layer(layers, body):
    for layer in range(layers):

        @pl.when(lax.axis_index("layer") == layer)
        def _():
            body(layer)


def clear_kernel(latent_ref, weight_ref, total_ref):
    total_ref[...] = jnp.zeros_like(total_ref)


def decode_chip_kernel(zero_ref, own_ref, core_ref, weight_ref, total_ref):
    layers = total_ref.shape[0]

    def body(layer):
        latents = [(layer, own_ref[...]), (layer ^ 1, core_ref[...])]
        for target in range(layers):
            reached = [entry for entry in latents if entry[0] <= target]
            if reached:
                total_ref[target] = products(reached, weight_ref, target)
            else:
                total_ref[target] = zero_ref[target]

    on_each_layer(layers, body)


def decode_more_kernel(offset, total_ref, latent_ref, weight_ref, out_ref):
    layers = total_ref.shape[0]

    def body(layer):
        source = layer ^ offset
        for target in range(layers):
            total = total_ref[target]
            if source <= target:
                total = total + products([(source, latent_ref[...])], weight_ref, target)
            out_ref[target] = total

    on_each_layer(layers, body)


def decode_last_kernel(total_ref, last_ref, weight_ref, out_ref):
    layers, tokens, _ = total_ref.shape

    def body(layer):
        source = layer ^ 2
        for target in range(layers):
            total = total_ref[target]
            if source <= target:
                total = total + products([(source, last_ref[...])], weight_ref, target)
            for token in range(tokens):
                out_ref[target * tokens + token] = total[token : token + 1, :]

    on_each_layer(layers, body)


def finish_kernel(parts_ref, bias_ref, out_ref):
    layers, shards, columns = parts_ref.shape[0], parts_ref.shape[1], parts_ref.shape[3]
    for block in range(layers):
        there = slice(block * columns, (block + 1) * columns)
        total = parts_ref[block, 0]
        for shard in range(1, shards):
            total = total + parts_ref[block, shard]
        out_ref[:, 0, there] = (total + bias_ref[:, there]).astype(out_ref.dtype)


def shards(resid_stream, enc_mantissa, enc_exponent, enc_bias, dec_weight, dec_bias):
    layer_count, feat_count = lax.axis_size("layer"), lax.axis_size("feat")
    tok_local, _, width = resid_stream.shape
    tokens = tok_local * feat_count
    feat_local = enc_mantissa.shape[2]
    col_local = dec_weight.shape[2]

    def place(layer, feat):
        return layer * feat_count + feat

    everywhere = [(layer, feat) for layer in range(layer_count) for feat in range(feat_count)]

    def swap(array, layer_bit=0, feat_bit=0, parities=(0, 1)):
        return lax.ppermute(
            array,
            AXES,
            [(place(l, f), place(l ^ layer_bit, f ^ feat_bit)) for l, f in everywhere if l % 2 in parities],
        )

    halves = 2 if width % (2 * BLK) == 0 else 1
    copies = kernel(
        prepare_kernel, jax.ShapeDtypeStruct((tokens, halves, width // halves), resid_stream.dtype), "prepare", work=20 * WORK
    )(resid_stream)
    gathered = lax.all_to_all(copies, "feat", 0, 0, tiled=True)
    latent = kernel(encode_kernel, jax.ShapeDtypeStruct((tokens, feat_local), jnp.bfloat16), "encode")(
        gathered, enc_mantissa[0], jnp.swapaxes(enc_exponent[0], 0, 1), enc_bias
    )
    weight = jnp.swapaxes(dec_weight, 1, 2)
    total = jax.ShapeDtypeStruct((layer_count, tokens, col_local), jnp.float32)
    other = swap(latent, layer_bit=3)
    zero = kernel(clear_kernel, total, "clear")(latent, weight)
    held, zero = lax.optimization_barrier((latent, zero))
    core = swap(held, layer_bit=1)
    same = swap(held, layer_bit=2)
    chip_total = kernel(decode_chip_kernel, total, "decode_chip")(zero, latent, core, weight)
    most_total = kernel(functools.partial(decode_more_kernel, 3), total, "decode_other")(chip_total, other, weight)
    parts = kernel(
        decode_last_kernel, jax.ShapeDtypeStruct((layer_count * tokens, 1, col_local), jnp.float32), "decode_same"
    )(most_total, same, weight)
    arrived = lax.all_to_all(parts, AXES, 0, 0, tiled=True)
    return kernel(finish_kernel, jax.ShapeDtypeStruct((tok_local, 1, width), jnp.bfloat16), "finish")(
        arrived.reshape(layer_count, feat_count, tok_local, col_local), dec_bias
    )


def solution(mesh):
    in_specs = (
        P("feat", "layer", None),
        P("layer", None, "feat"),
        P("layer", None, "feat"),
        P("layer", "feat"),
        P(None, "feat", "layer"),
        P("layer", None),
    )
    out_specs = P("feat", "layer", None)
    return jax.shard_map(shards, mesh=mesh, in_specs=in_specs, out_specs=out_specs, check_vma=False)
```

```python
import functools

import jax
import jax.numpy as jnp
from jax import lax
from jax.experimental import pallas as pl
from jax.experimental.pallas import tpu as pltpu
from jax.sharding import PartitionSpec as P

BLK = 128
AXES = ("layer", "feat")
VMEM = pl.BlockSpec(memory_space=pltpu.VMEM)
LIMIT = 8 * 1024 * 1024
WORK = 2_000_000_000
OVER_ROWS = (((1,), (1,)), ((), ()))


def kernel(body, out_shape, name, scratch_shapes=(), work=WORK):
    def call(*operands):
        return pl.pallas_call(
            body,
            out_shape=out_shape,
            in_specs=[VMEM] * len(operands),
            out_specs=VMEM,
            scratch_shapes=scratch_shapes,
            compiler_params=pltpu.CompilerParams(vmem_limit_bytes=LIMIT),
            cost_estimate=pl.CostEstimate(flops=work, bytes_accessed=0, transcendentals=0),
            name=name,
        )(*operands)

    return call


def prepare_kernel(own_ref, copies_ref):
    _, parts, columns = copies_ref.shape
    own = own_ref[0].astype(jnp.float32)
    rows = [own[:, part * columns : (part + 1) * columns] for part in range(parts)]
    own = jnp.concatenate(rows, axis=0).astype(copies_ref.dtype)
    for copy in range(copies_ref.shape[0]):
        copies_ref[copy] = own


def encode_kernel(all_ref, mantissa_ref, exponent_ref, bias_ref, latent_ref):
    parts = all_ref[...].astype(jnp.float32)
    x = jnp.concatenate([parts[:, part, :] for part in range(parts.shape[1])], axis=1)
    tokens, width = x.shape
    blocks, rows = exponent_ref.shape
    scale = jnp.exp2(exponent_ref[...].astype(jnp.float32)).astype(jnp.bfloat16)
    row_of = lax.broadcasted_iota(jnp.int32, (rows, width), 1) // BLK
    spread = (row_of == lax.broadcasted_iota(jnp.int32, (rows, width), 0)).astype(jnp.bfloat16)
    scales = jnp.dot(scale, spread, preferred_element_type=jnp.float32)
    for first in range(0, blocks, 2):
        group = range(first, min(first + 2, blocks))
        scaled = jnp.concatenate([x * scales[j : j + 1, :] for j in group], axis=0).astype(jnp.bfloat16)
        columns = slice(first * BLK, (first + len(group)) * BLK)
        product = jnp.dot(scaled, mantissa_ref[:, columns], preferred_element_type=jnp.float32)
        for at, j in enumerate(group):
            own = product[at * tokens : (at + 1) * tokens, at * BLK : (at + 1) * BLK]
            there = slice(j * BLK, (j + 1) * BLK)
            latent_ref[:, there] = jnp.maximum(own + bias_ref[:, there], 0.0).astype(latent_ref.dtype)


def products(latents, weight_ref, target):
    columns, features = weight_ref.shape[1:]
    still, step = columns // 512 * 256, min(features, 256)
    fixed, moved = None, None
    for source, latent in latents:
        pair = target * (target + 1) // 2 + source
        for at in range(0, features, step):
            there = slice(at, at + step)
            if still:
                part = lax.dot_general(
                    latent[:, there], weight_ref[pair, :still, there], OVER_ROWS, preferred_element_type=jnp.float32
                )
                fixed = part if fixed is None else fixed + part
            part = lax.dot_general(
                weight_ref[pair, still:, there], latent[:, there], OVER_ROWS, preferred_element_type=jnp.float32
            )
            moved = part if moved is None else moved + part
    return jnp.concatenate([fixed, moved.T], axis=1) if still else moved.T


def on_each_layer(layers, body):
    for layer in range(layers):

        @pl.when(lax.axis_index("layer") == layer)
        def _():
            body(layer)


def clear_kernel(latent_ref, weight_ref, total_ref):
    total_ref[...] = jnp.zeros_like(total_ref)


def decode_chip_kernel(zero_ref, own_ref, core_ref, weight_ref, total_ref):
    layers = total_ref.shape[0]

    def body(layer):
        latents = [(layer, own_ref[...]), (layer ^ 1, core_ref[...])]
        for target in range(layers):
            reached = [entry for entry in latents if entry[0] <= target]
            if reached:
                total_ref[target] = products(reached, weight_ref, target)
            else:
                total_ref[target] = zero_ref[target]

    on_each_layer(layers, body)


def decode_more_kernel(offset, total_ref, latent_ref, weight_ref, out_ref):
    layers = total_ref.shape[0]

    def body(layer):
        source = layer ^ offset
        for target in range(layers):
            total = total_ref[target]
            if source <= target:
                total = total + products([(source, latent_ref[...])], weight_ref, target)
            out_ref[target] = total

    on_each_layer(layers, body)


def decode_last_kernel(total_ref, last_ref, weight_ref, out_ref):
    layers, tokens, _ = total_ref.shape

    def body(layer):
        source = layer ^ 2
        for target in range(layers):
            total = total_ref[target]
            if source <= target:
                total = total + products([(source, last_ref[...])], weight_ref, target)
            piece = out_ref.shape[2]
            rest = 2 * piece - total.shape[1]
            first = total[:, :piece]
            second = jnp.concatenate([total[:, piece:], jnp.zeros((tokens, rest), total.dtype)], axis=1)
            for token in range(tokens):
                rows = jnp.concatenate([first[token : token + 1, :], second[token : token + 1, :]], axis=0)
                out_ref[target * tokens + token] = rows.astype(out_ref.dtype)

    on_each_layer(layers, body)


def finish_kernel(columns, parts_ref, bias_ref, out_ref):
    layers, shards, _, piece = parts_ref.shape
    for block in range(layers):
        total = parts_ref[block, 0].astype(jnp.float32)
        for shard in range(1, shards):
            total = total + parts_ref[block, shard].astype(jnp.float32)
        for row, start, stop in ((0, 0, piece), (1, piece, columns)):
            there = slice(block * columns + start, block * columns + stop)
            out_ref[:, 0, there] = (total[row : row + 1, : stop - start] + bias_ref[:, there]).astype(out_ref.dtype)


def shards(resid_stream, enc_mantissa, enc_exponent, enc_bias, dec_weight, dec_bias):
    layer_count, feat_count = lax.axis_size("layer"), lax.axis_size("feat")
    tok_local, _, width = resid_stream.shape
    tokens = tok_local * feat_count
    feat_local = enc_mantissa.shape[2]
    col_local = dec_weight.shape[2]

    def place(layer, feat):
        return layer * feat_count + feat

    everywhere = [(layer, feat) for layer in range(layer_count) for feat in range(feat_count)]

    def swap(array, layer_bit=0, feat_bit=0, parities=(0, 1)):
        return lax.ppermute(
            array,
            AXES,
            [(place(l, f), place(l ^ layer_bit, f ^ feat_bit)) for l, f in everywhere if l % 2 in parities],
        )

    halves = 2 if width % (2 * BLK) == 0 else 1
    piece = -(-col_local // (2 * BLK)) * BLK
    copies = kernel(
        prepare_kernel, jax.ShapeDtypeStruct((tokens, halves, width // halves), resid_stream.dtype), "prepare", work=20 * WORK
    )(resid_stream)
    gathered = lax.all_to_all(copies, "feat", 0, 0, tiled=True)
    latent = kernel(encode_kernel, jax.ShapeDtypeStruct((tokens, feat_local), jnp.bfloat16), "encode")(
        gathered, enc_mantissa[0], jnp.swapaxes(enc_exponent[0], 0, 1), enc_bias
    )
    weight = jnp.swapaxes(dec_weight, 1, 2)
    total = jax.ShapeDtypeStruct((layer_count, tokens, col_local), jnp.float32)
    other = swap(latent, layer_bit=3)
    zero = kernel(clear_kernel, total, "clear")(latent, weight)
    held, zero = lax.optimization_barrier((latent, zero))
    core = swap(held, layer_bit=1)
    same = swap(held, layer_bit=2)
    chip_total = kernel(decode_chip_kernel, total, "decode_chip")(zero, latent, core, weight)
    most_total = kernel(functools.partial(decode_more_kernel, 3), total, "decode_other")(chip_total, other, weight)
    parts = kernel(
        decode_last_kernel, jax.ShapeDtypeStruct((layer_count * tokens, 2, piece), jnp.bfloat16), "decode_same"
    )(most_total, same, weight)
    arrived = lax.all_to_all(parts, AXES, 0, 0, tiled=True)
    return kernel(functools.partial(finish_kernel, col_local), jax.ShapeDtypeStruct((tok_local, 1, width), jnp.bfloat16), "finish")(
        arrived.reshape(layer_count, feat_count, 2, piece), dec_bias
    )


def solution(mesh):
    in_specs = (
        P("feat", "layer", None),
        P("layer", None, "feat"),
        P("layer", None, "feat"),
        P("layer", "feat"),
        P(None, "feat", "layer"),
        P("layer", None),
    )
    out_specs = P("feat", "layer", None)
    return jax.shard_map(shards, mesh=mesh, in_specs=in_specs, out_specs=out_specs, check_vma=False)
```

```python
import functools

import jax
import jax.numpy as jnp
from jax import lax
from jax.experimental import pallas as pl
from jax.experimental.pallas import tpu as pltpu
from jax.sharding import PartitionSpec as P

BLK = 128
AXES = ("layer", "feat")
VMEM = pl.BlockSpec(memory_space=pltpu.VMEM)
LIMIT = 8 * 1024 * 1024
WORK = 2_000_000_000
OVER_ROWS = (((1,), (1,)), ((), ()))


def kernel(body, out_shape, name, scratch_shapes=(), work=WORK):
    def call(*operands):
        return pl.pallas_call(
            body,
            out_shape=out_shape,
            in_specs=[VMEM] * len(operands),
            out_specs=VMEM,
            scratch_shapes=scratch_shapes,
            compiler_params=pltpu.CompilerParams(vmem_limit_bytes=LIMIT),
            cost_estimate=pl.CostEstimate(flops=work, bytes_accessed=0, transcendentals=0),
            name=name,
        )(*operands)

    return call


def take_kernel(own_ref, out_ref):
    out_ref[...] = own_ref[...]


def prepare_kernel(own_ref, copies_ref):
    _, parts, columns = copies_ref.shape
    own = own_ref[0].astype(jnp.float32)
    rows = [own[:, part * columns : (part + 1) * columns] for part in range(parts)]
    own = jnp.concatenate(rows, axis=0).astype(copies_ref.dtype)
    for copy in range(copies_ref.shape[0]):
        copies_ref[copy] = own


def encode_kernel(all_ref, mantissa_ref, exponent_ref, bias_ref, latent_ref):
    parts = all_ref[...].astype(jnp.float32)
    x = jnp.concatenate([parts[:, part, :] for part in range(parts.shape[1])], axis=1)
    tokens, width = x.shape
    blocks, rows = exponent_ref.shape
    scale = jnp.exp2(exponent_ref[...].astype(jnp.float32)).astype(jnp.bfloat16)
    row_of = lax.broadcasted_iota(jnp.int32, (rows, width), 1) // BLK
    spread = (row_of == lax.broadcasted_iota(jnp.int32, (rows, width), 0)).astype(jnp.bfloat16)
    scales = jnp.dot(scale, spread, preferred_element_type=jnp.float32)
    for first in range(0, blocks, 2):
        group = range(first, min(first + 2, blocks))
        scaled = jnp.concatenate([x * scales[j : j + 1, :] for j in group], axis=0).astype(jnp.bfloat16)
        columns = slice(first * BLK, (first + len(group)) * BLK)
        product = jnp.dot(scaled, mantissa_ref[:, columns], preferred_element_type=jnp.float32)
        for at, j in enumerate(group):
            own = product[at * tokens : (at + 1) * tokens, at * BLK : (at + 1) * BLK]
            there = slice(j * BLK, (j + 1) * BLK)
            latent_ref[:, there] = jnp.maximum(own + bias_ref[:, there], 0.0).astype(latent_ref.dtype)


def products(latents, weight_ref, target):
    columns, features = weight_ref.shape[1:]
    still, step = columns // 512 * 256, min(features, 256)
    fixed, moved = None, None
    for source, latent in latents:
        pair = target * (target + 1) // 2 + source
        for at in range(0, features, step):
            there = slice(at, at + step)
            if still:
                part = lax.dot_general(
                    latent[:, there], weight_ref[pair, :still, there], OVER_ROWS, preferred_element_type=jnp.float32
                )
                fixed = part if fixed is None else fixed + part
            part = lax.dot_general(
                weight_ref[pair, still:, there], latent[:, there], OVER_ROWS, preferred_element_type=jnp.float32
            )
            moved = part if moved is None else moved + part
    return jnp.concatenate([fixed, moved.T], axis=1) if still else moved.T


def on_each_layer(layers, body):
    for layer in range(layers):

        @pl.when(lax.axis_index("layer") == layer)
        def _():
            body(layer)


def clear_kernel(latent_ref, weight_ref, total_ref):
    total_ref[...] = jnp.zeros_like(total_ref)


def decode_chip_kernel(zero_ref, own_ref, core_ref, weight_ref, total_ref):
    layers = total_ref.shape[0]

    def body(layer):
        latents = [(layer, own_ref[...]), (layer ^ 1, core_ref[...])]
        for target in range(layers):
            reached = [entry for entry in latents if entry[0] <= target]
            if reached:
                total_ref[target] = products(reached, weight_ref, target)
            else:
                total_ref[target] = zero_ref[target]

    on_each_layer(layers, body)


def decode_more_kernel(offset, total_ref, latent_ref, weight_ref, out_ref):
    layers = total_ref.shape[0]

    def body(layer):
        source = layer ^ offset
        for target in range(layers):
            total = total_ref[target]
            if source <= target:
                total = total + products([(source, latent_ref[...])], weight_ref, target)
            out_ref[target] = total

    on_each_layer(layers, body)


def decode_last_kernel(total_ref, last_ref, weight_ref, out_ref):
    layers, tokens, _ = total_ref.shape

    def body(layer):
        source = layer ^ 2
        for target in range(layers):
            total = total_ref[target]
            if source <= target:
                total = total + products([(source, last_ref[...])], weight_ref, target)
            for token in range(tokens):
                out_ref[target * tokens + token] = total[token : token + 1, :]

    on_each_layer(layers, body)


def finish_kernel(parts_ref, bias_ref, out_ref):
    layers, shards, columns = parts_ref.shape[0], parts_ref.shape[1], parts_ref.shape[3]
    for block in range(layers):
        there = slice(block * columns, (block + 1) * columns)
        total = parts_ref[block, 0]
        for shard in range(1, shards):
            total = total + parts_ref[block, shard]
        out_ref[:, 0, there] = (total + bias_ref[:, there]).astype(out_ref.dtype)


def shards(resid_stream, enc_mantissa, enc_exponent, enc_bias, dec_weight, dec_bias):
    layer_count, feat_count = lax.axis_size("layer"), lax.axis_size("feat")
    tok_local, _, width = resid_stream.shape
    tokens = tok_local * feat_count
    feat_local = enc_mantissa.shape[2]
    col_local = dec_weight.shape[2]

    def place(layer, feat):
        return layer * feat_count + feat

    everywhere = [(layer, feat) for layer in range(layer_count) for feat in range(feat_count)]

    def swap(array, layer_bit=0, feat_bit=0, parities=(0, 1)):
        return lax.ppermute(
            array,
            AXES,
            [(place(l, f), place(l ^ layer_bit, f ^ feat_bit)) for l, f in everywhere if l % 2 in parities],
        )

    own = kernel(take_kernel, jax.ShapeDtypeStruct(resid_stream.shape, resid_stream.dtype), "take", work=1000)(resid_stream)
    halves = 2 if width % (2 * BLK) == 0 else 1
    copies = kernel(
        prepare_kernel, jax.ShapeDtypeStruct((tokens, halves, width // halves), resid_stream.dtype), "prepare", work=7 * WORK
    )(own)
    gathered = lax.all_to_all(copies, "feat", 0, 0, tiled=True)
    latent = kernel(encode_kernel, jax.ShapeDtypeStruct((tokens, feat_local), jnp.bfloat16), "encode")(
        gathered, enc_mantissa[0], jnp.swapaxes(enc_exponent[0], 0, 1), enc_bias
    )
    weight = jnp.swapaxes(dec_weight, 1, 2)
    total = jax.ShapeDtypeStruct((layer_count, tokens, col_local), jnp.float32)
    other = swap(latent, layer_bit=3)
    zero = kernel(clear_kernel, total, "clear")(latent, weight)
    held, zero = lax.optimization_barrier((latent, zero))
    core = swap(held, layer_bit=1)
    same = swap(held, layer_bit=2)
    chip_total = kernel(decode_chip_kernel, total, "decode_chip")(zero, latent, core, weight)
    most_total = kernel(functools.partial(decode_more_kernel, 3), total, "decode_other")(chip_total, other, weight)
    parts = kernel(
        decode_last_kernel, jax.ShapeDtypeStruct((layer_count * tokens, 1, col_local), jnp.float32), "decode_same"
    )(most_total, same, weight)
    arrived = lax.all_to_all(parts, AXES, 0, 0, tiled=True)
    return kernel(finish_kernel, jax.ShapeDtypeStruct((tok_local, 1, width), jnp.bfloat16), "finish")(
        arrived.reshape(layer_count, feat_count, tok_local, col_local), dec_bias
    )


def solution(mesh):
    in_specs = (
        P("feat", "layer", None),
        P("layer", None, "feat"),
        P("layer", None, "feat"),
        P("layer", "feat"),
        P(None, "feat", "layer"),
        P("layer", None),
    )
    out_specs = P("feat", "layer", None)
    return jax.shard_map(shards, mesh=mesh, in_specs=in_specs, out_specs=out_specs, check_vma=False)
```
